512 devices in a mesh: tm: 32 (over x_lo, z), gx: 16 (over x_hi, y, core).
Axes of the slice: x: 4 (x_hi: 2, x_lo: 2; x = x_hi * 2 + x_lo), y: 4, z: 16, core: 2. Of those that a mesh axis runs over, the one named last changes fastest.
Arguments:
- initial: float32 [32, 256, 256], P('gx'), may hold values from -1 to 1
- node_values: float32 [32, 3, 32, 256, 256], P('tm', None, 'gx'), may hold values from -1 to 1
Outputs:
- solution: float32 [32, 3, 32, 256, 256], P('tm', None, 'gx')
The draws below stay inside these ranges and needn't reach their ends.
All inputs are finite; a program needn't handle non-finite values.
Results may differ from the reference program's by a relative error of at most 0.0002.
Values sent between devices are 32-bit elements; how exact they have to be, the bound alone decides.
A program may use at most 64 MiB of HBM per device.

```python
import math
import jax
import jax.numpy as jnp
from jax import lax

NY = 256
NZ = 256
NODES = 3
SWEEPS = 2
NX = 32
TSL = 32


def checker_field(key, shape):
    count = len(shape)
    parity_sum = lax.broadcasted_iota(jnp.int32, shape, count - 3) + lax.broadcasted_iota(jnp.int32, shape, count - 2) + lax.broadcasted_iota(jnp.int32, shape, count - 1)
    sign_field = jnp.where(parity_sum % 2 == 0, 1.0, -1.0).astype(jnp.float32)
    low_end = 0.5
    amplitude = jax.random.uniform(key, shape, jnp.float32, low_end, 1.0)
    return (sign_field * amplitude).astype(jnp.float32)


def draw_initial(key, part):
    return checker_field(jax.random.fold_in(key, 11), (NX, NY, NZ))


def draw_node_values(key, part):
    return checker_field(jax.random.fold_in(key, 23), (TSL, NODES, NX, NY, NZ))


def setup_inputs(seed: int = 0) -> dict:
    key_of = jax.random.split(jax.random.key(seed), 3)
    return {
        "initial": draw_initial(jax.random.fold_in(key_of[2], 71), 0),
        "node_values": draw_node_values(jax.random.fold_in(key_of[2], 71), 0),
    }


spacing = 2.0
step_size = 0.2
half_step = 0.1


def second_derivative(count):
    positions = jnp.arange(count, dtype=jnp.int32)
    offset = positions[None, :] - positions[:, None]
    angle_step = 2.0 * math.pi / count
    parity = jnp.where(offset % 2 == 0, 1.0, -1.0).astype(jnp.float32)
    safe = jnp.where(offset == 0, 1, offset).astype(jnp.float32)
    sine_value = jnp.sin(safe * (angle_step / 2.0))
    off_value = -0.5 * parity / (sine_value * sine_value)
    diagonal_value = -(math.pi ** 2) / (3.0 * angle_step * angle_step) - 1.0 / 6.0
    matrix = jnp.where(offset == 0, jnp.float32(diagonal_value), off_value)
    return (matrix * (angle_step / spacing) ** 2).astype(jnp.float32)


def evaluate(state_field, matrix_y, matrix_z):
    across = (-(jnp.roll(state_field, 2, 1) + jnp.roll(state_field, -2, 1))
              + 16.0 * (jnp.roll(state_field, 1, 1) + jnp.roll(state_field, -1, 1))
              - 30.0 * state_field) / 12.0
    term_y = jnp.einsum('jk,txkz->txjz', matrix_y, state_field, precision=lax.Precision.HIGHEST)
    term_z = jnp.einsum('txyk,kz->txyz', state_field, matrix_z, precision=lax.Precision.HIGHEST)
    return across + term_y + term_z + state_field - state_field * state_field * state_field


def reference(initial, node_values):
    matrix_y = second_derivative(NY)
    matrix_z = second_derivative(NZ)
    values = [node_values[:, 0], node_values[:, 1], node_values[:, 2]]
    forces = [evaluate(item, matrix_y, matrix_z) for item in values]
    for sweep_index in range(SWEEPS):
        quadrature_one = step_size * (5.0 / 24.0 * forces[0] + 1.0 / 3.0 * forces[1] - 1.0 / 24.0 * forces[2])
        quadrature_two = step_size * (-1.0 / 24.0 * forces[0] + 1.0 / 3.0 * forces[1] + 5.0 / 24.0 * forces[2])
        first_node = jnp.concatenate([initial[None], values[2][:-1]], axis=0)
        first_force = evaluate(first_node, matrix_y, matrix_z)
        middle = first_node + half_step * (first_force - forces[0]) + quadrature_one
        middle_force = evaluate(middle, matrix_y, matrix_z)
        final_node = middle + half_step * (middle_force - forces[1]) + quadrature_two
        final_force = evaluate(final_node, matrix_y, matrix_z)
        values = [first_node, middle, final_node]
        forces = [first_force, middle_force, final_force]
    return jnp.stack(values, axis=1)
```

```python
import math

import jax
import jax.numpy as jnp
import numpy as np
from jax import lax
from jax.experimental import pallas as pl
from jax.experimental.pallas import tpu as pltpu
from jax.sharding import PartitionSpec as P

MESH = pl.DeviceIdType.MESH

SPACING = 2.0
STEP = 0.2
HALF = 0.1
CHUNKS = 8

FIRST = (-HALF + STEP * 5.0 / 24.0, STEP / 3.0, -STEP / 24.0)
SECOND = (-STEP / 24.0, -HALF + STEP / 3.0, STEP * 5.0 / 24.0)


def second_derivative(count):
    positions = np.arange(count)
    offset = positions[None, :] - positions[:, None]
    angle_step = 2.0 * math.pi / count
    parity = np.where(offset % 2 == 0, 1.0, -1.0)
    safe = np.where(offset == 0, 1, offset)
    off_value = -0.5 * parity / np.sin(safe * (angle_step / 2.0)) ** 2
    diagonal = -(math.pi**2) / (3.0 * angle_step * angle_step) - 1.0 / 6.0
    return np.where(offset == 0, diagonal, off_value) * (angle_step / SPACING) ** 2


def split(x):
    high = x.astype(jnp.bfloat16)
    low = (x - high.astype(jnp.float32)).astype(jnp.bfloat16)
    return high, low


def dot(a, b):
    return jnp.dot(a, b, preferred_element_type=jnp.float32)


def reaction(v):
    return v - v * v * v


def kernel(
    nt,
    ng,
    initial,
    nodes,
    q_high,
    q_low,
    out,
    u0,
    u1,
    u2,
    a0,
    b0,
    w,
    halo,
    w_high,
    w_low,
    r1,
    m1,
    r2,
    m2,
    base,
    qterm,
    load_sem,
    start_sem,
    relay_send,
    relay_recv,
    halo_send,
    halo_recv,
    store_sem,
):
    t = lax.axis_index("tm")
    g = lax.axis_index("gx")
    right = lax.rem(g + 1, ng)
    left = lax.rem(g + ng - 1, ng)
    planes, ny, nz = u0.shape
    rows = ny // CHUNKS

    def part(c):
        return pl.ds(pl.multiple_of(c * rows, rows), rows)

    loads = [
        pltpu.make_async_copy(nodes.at[0, m], u, load_sem.at[m])
        for m, u in enumerate((u0, u1, u2))
    ]
    for load in loads:
        load.start()

    starts = [
        pltpu.make_async_copy(initial, a, start_sem.at[i])
        for i, a in enumerate((a0, b0))
    ]

    @pl.when(t == 0)
    def _():
        for start in starts:
            start.start()

    barrier = pltpu.get_barrier_semaphore()
    for side in (left, right):
        pl.semaphore_signal(barrier, inc=1, device_id=(t, side), device_id_type=MESH)

    @pl.when(t > 0)
    def _():
        pl.semaphore_signal(barrier, inc=1, device_id=(t - 1, g), device_id_type=MESH)

    pl.semaphore_wait(barrier, jnp.where(t < nt - 1, 3, 2))

    def relay(sweep, c):
        source = nodes.at[0, 2, :, part(c), :] if sweep == 0 else u2.at[:, part(c), :]
        target = (a0, b0)[sweep].at[:, part(c), :]
        return pltpu.make_async_remote_copy(
            source,
            target,
            relay_send.at[sweep, c],
            relay_recv.at[sweep, c],
            device_id=(t + 1, g),
            device_id_type=MESH,
        )

    def exchange(stage, side, c):
        return pltpu.make_async_remote_copy(
            w.at[stage, :, part(c), :],
            halo.at[stage, side, :, part(c), :],
            halo_send.at[stage, side, c],
            halo_recv.at[stage, side, c],
            device_id=(t, (right, left)[side]),
            device_id_type=MESH,
        )

    def loop(body):
        lax.fori_loop(0, CHUNKS, lambda c, _: (body(c), 0)[1], 0)

    @pl.when(t < nt - 1)
    def _():
        loop(lambda c: relay(0, c).start())

    for load in loads:
        load.wait()

    def prepare(c, first, middle, last):
        rhs = [reaction(first), reaction(middle), reaction(last)]
        old = (first, middle, last)
        at = (slice(None), part(c), slice(None))
        r1[at] = sum(k * v for k, v in zip(FIRST, old))
        m1[at] = sum(k * v for k, v in zip(FIRST, rhs))
        r2[at] = sum(k * v for k, v in zip(SECOND, old))
        m2[at] = sum(k * v for k, v in zip(SECOND, rhs))

    def across(stage, c):
        here = w[stage, :, part(c), :]
        before = halo[stage, 0, :, part(c), :]
        after = halo[stage, 1, :, part(c), :]
        one = 16.0 * (before[1] + here[1]) - 30.0 * here[0] - (before[0] + after[0])
        two = 16.0 * (here[0] + after[0]) - 30.0 * here[1] - (before[1] + after[1])
        return jnp.stack([one, two]) * (1.0 / 12.0)

    def offer(stage, c, value):
        w[stage, :, part(c), :] = value
        exchange(stage, 0, c).start()
        exchange(stage, 1, c).start()
        high, low = split(value)
        w_high[:, part(c), :] = high
        w_low[:, part(c), :] = low
        high = high.reshape(planes * rows, nz)
        low = low.reshape(planes * rows, nz)
        product = dot(high, q_high[...]) + dot(low, q_high[...]) + dot(high, q_low[...])
        qterm[:, part(c), :] = product.reshape(planes, rows, nz)

    def product_rows():
        for p in range(planes):
            qterm[p] += (
                dot(q_high[...], w_high[p])
                + dot(q_high[...], w_low[p])
                + dot(q_low[...], w_high[p])
            )

    def arrive(stage, c):
        exchange(stage, 0, c).wait_recv()
        exchange(stage, 1, c).wait_recv()

    loop(
        lambda c: prepare(
            c, u0[:, part(c), :], u1[:, part(c), :], u2[:, part(c), :]
        )
    )

    for sweep in range(2):
        begin = (a0, b0)[sweep]
        one, two = 2 * sweep, 2 * sweep + 1

        @pl.when(t == 0)
        def _():
            starts[sweep].wait()

        def take(c):
            @pl.when(t > 0)
            def _():
                relay(sweep, c).wait_recv()

            value = begin[:, part(c), :]
            base[:, part(c), :] = value + HALF * reaction(value) + m1[:, part(c), :]
            offer(one, c, HALF * value + r1[:, part(c), :])

        loop(take)
        if sweep == 1:
            pltpu.make_async_copy(b0, out.at[0, 0], store_sem.at[0]).start()
        product_rows()

        def middle(c):
            arrive(one, c)
            value = base[:, part(c), :] + qterm[:, part(c), :] + across(one, c)
            u1[:, part(c), :] = value
            base[:, part(c), :] = value + HALF * reaction(value) + m2[:, part(c), :]
            offer(two, c, HALF * value + r2[:, part(c), :])

        loop(middle)
        if sweep == 1:
            pltpu.make_async_copy(u1, out.at[0, 1], store_sem.at[1]).start()
        product_rows()

        def final(c):
            arrive(two, c)
            value = base[:, part(c), :] + qterm[:, part(c), :] + across(two, c)
            if sweep == 0:
                u2[:, part(c), :] = value

                @pl.when(t < nt - 1)
                def _():
                    relay(1, c).start()

                prepare(c, a0[:, part(c), :], u1[:, part(c), :], value)
            else:
                u0[:, part(c), :] = value

        if sweep == 0:

            @pl.when(t < nt - 1)
            def _():
                loop(lambda c: relay(0, c).wait_send())

        loop(final)

    last = pltpu.make_async_copy(u0, out.at[0, 2], store_sem.at[2])
    last.start()

    def drain(c):
        for stage in range(4):
            for side in range(2):
                exchange(stage, side, c).wait_send()

    loop(drain)

    @pl.when(t < nt - 1)
    def _():
        loop(lambda c: relay(1, c).wait_send())

    pltpu.make_async_copy(b0, out.at[0, 0], store_sem.at[0]).wait()
    pltpu.make_async_copy(u1, out.at[0, 1], store_sem.at[1]).wait()
    last.wait()


def solution(mesh):
    nt, ng = mesh.shape["tm"], mesh.shape["gx"]

    def local(initial, nodes):
        planes, ny, nz = initial.shape
        exact = second_derivative(ny).astype(np.float32)
        q_high = exact.astype(jnp.bfloat16)
        q_low = (exact - q_high.astype(np.float32)).astype(jnp.bfloat16)
        field = pltpu.VMEM((planes, ny, nz), jnp.float32)
        half_field = pltpu.VMEM((planes, ny, nz), jnp.bfloat16)
        dma = pltpu.SemaphoreType.DMA
        hbm = pl.BlockSpec(memory_space=pl.ANY)
        vmem = pl.BlockSpec(memory_space=pltpu.VMEM)

        def body(*refs):
            kernel(nt, ng, *refs)

        return pl.pallas_call(
            body,
            out_shape=jax.ShapeDtypeStruct(nodes.shape, nodes.dtype),
            in_specs=[hbm, hbm, vmem, vmem],
            out_specs=hbm,
            scratch_shapes=[
                field,
                field,
                field,
                field,
                field,
                pltpu.VMEM((4, planes, ny, nz), jnp.float32),
                pltpu.VMEM((4, 2, planes, ny, nz), jnp.float32),
                half_field,
                half_field,
                field,
                field,
                field,
                field,
                field,
                field,
                dma((3,)),
                dma((2,)),
                dma((2, CHUNKS)),
                dma((2, CHUNKS)),
                dma((4, 2, CHUNKS)),
                dma((4, 2, CHUNKS)),
                dma((3,)),
            ],
            compiler_params=pltpu.CompilerParams(
                collective_id=0,
                has_side_effects=True,
                vmem_limit_bytes=40 * 1024 * 1024,
            ),
            name="sweeps",
        )(initial, nodes, jnp.asarray(q_high), jnp.asarray(q_low))

    in_specs = (P("gx", None, None), P("tm", None, "gx", None, None))
    out_specs = P("tm", None, "gx", None, None)
    return jax.shard_map(
        local, mesh=mesh, in_specs=in_specs, out_specs=out_specs, check_vma=False
    )
```

```python
import math

import jax
import jax.numpy as jnp
import numpy as np
from jax import lax
from jax.experimental import pallas as pl
from jax.experimental.pallas import tpu as pltpu
from jax.sharding import PartitionSpec as P

MESH = pl.DeviceIdType.MESH

SPACING = 2.0
STEP = 0.2
HALF = 0.1
PARTS = 8
FINE = 8

FIRST = (-HALF + STEP * 5.0 / 24.0, STEP / 3.0, -STEP / 24.0)
SECOND = (-STEP / 24.0, -HALF + STEP / 3.0, STEP * 5.0 / 24.0)


def second_derivative(count):
    positions = np.arange(count)
    offset = positions[None, :] - positions[:, None]
    angle_step = 2.0 * math.pi / count
    parity = np.where(offset % 2 == 0, 1.0, -1.0)
    safe = np.where(offset == 0, 1, offset)
    off_value = -0.5 * parity / np.sin(safe * (angle_step / 2.0)) ** 2
    diagonal = -(math.pi**2) / (3.0 * angle_step * angle_step) - 1.0 / 6.0
    return np.where(offset == 0, diagonal, off_value) * (angle_step / SPACING) ** 2


def split(x):
    high = x.astype(jnp.bfloat16)
    low = (x - high.astype(jnp.float32)).astype(jnp.bfloat16)
    return high, low


def dot(a, b):
    return jnp.dot(a, b, preferred_element_type=jnp.float32)


def reaction(v):
    return v - v * v * v


def kernel(
    nt,
    ng,
    initial,
    nodes,
    q_high_in,
    q_low_in,
    out,
    u0,
    u1,
    u2,
    a0,
    b0,
    passing,
    w,
    halo,
    w_high,
    w_low,
    q_high,
    q_low,
    r1,
    m1,
    r2,
    m2,
    base,
    qterm,
    load_sem,
    start_sem,
    relay_send,
    relay_recv,
    pass_recv,
    halo_send,
    halo_recv,
):
    t = lax.axis_index("tm")
    g = lax.axis_index("gx")
    right = lax.rem(g + 1, ng)
    left = lax.rem(g + ng - 1, ng)
    planes, ny, nz = u0.shape
    rows, fine_rows = ny // PARTS, ny // FINE
    ratio = FINE // PARTS
    turn = nt // 2

    def part(c):
        return pl.ds(pl.multiple_of(c * rows, rows), rows)

    def fine(c):
        return pl.ds(pl.multiple_of(c * fine_rows, fine_rows), fine_rows)

    loads = [
        pltpu.make_async_copy(nodes.at[0, m], u, load_sem.at[m])
        for m, u in enumerate((u0, u1, u2))
    ]
    loads += [
        pltpu.make_async_copy(q_high_in, q_high, load_sem.at[3]),
        pltpu.make_async_copy(q_low_in, q_low, load_sem.at[4]),
    ]
    for load in loads:
        load.start()

    starts = [
        pltpu.make_async_copy(initial, a, start_sem.at[i])
        for i, a in enumerate((a0, b0))
    ]

    @pl.when(t == 0)
    def _():
        for start in starts:
            start.start()

    barrier = pltpu.get_barrier_semaphore()
    for side in (left, right):
        pl.semaphore_signal(barrier, inc=1, device_id=(t, side), device_id_type=MESH)

    @pl.when(t > 0)
    def _():
        pl.semaphore_signal(barrier, inc=1, device_id=(t - 1, g), device_id_type=MESH)

    @pl.when(t == turn)
    def _():
        pl.semaphore_signal(barrier, inc=1, device_id=(nt - 1, g), device_id_type=MESH)

    @pl.when(t == nt - 1)
    def _():
        pl.semaphore_signal(barrier, inc=1, device_id=(turn - 1, g), device_id_type=MESH)

    pl.semaphore_wait(barrier, jnp.where(t == turn - 1, 4, 3))

    def relay(sweep, c):
        source = nodes.at[0, 2, :, fine(c), :] if sweep == 0 else u2.at[:, fine(c), :]
        target = (a0, b0)[sweep].at[:, fine(c), :]
        return pltpu.make_async_remote_copy(
            source,
            target,
            relay_send.at[sweep, c],
            relay_recv.at[sweep, c],
            device_id=(t + 1, g),
            device_id_type=MESH,
        )

    def detour(sweep, c):
        source = nodes.at[0, 2, :, fine(c), :] if sweep == 0 else u2.at[:, fine(c), :]
        return pltpu.make_async_remote_copy(
            source,
            passing.at[sweep, :, fine(c), :],
            relay_send.at[sweep, c],
            pass_recv.at[sweep, c],
            device_id=(nt - 1, g),
            device_id_type=MESH,
        )

    def forward(sweep, c):
        return pltpu.make_async_remote_copy(
            passing.at[sweep, :, fine(c), :],
            (a0, b0)[sweep].at[:, fine(c), :],
            relay_send.at[sweep, c],
            relay_recv.at[sweep, c],
            device_id=(turn, g),
            device_id_type=MESH,
        )

    def aside(c):
        return (lax.rem(c, 2 * ratio) < ratio) & (c < 3 * FINE // 4)

    def give(sweep, c):
        around = (t == turn - 1) & aside(c)

        @pl.when(around)
        def _():
            detour(sweep, c).start()

        @pl.when((t < nt - 1) & ~around)
        def _():
            relay(sweep, c).start()

    def pass_on(sweep, k, due):
        @pl.when((t == nt - 1) & due)
        def _():
            for i in range(ratio):
                detour(sweep, k * ratio + i).wait_recv()
                forward(sweep, k * ratio + i).start()

    def given(sweep, c):
        @pl.when((t < nt - 1) | aside(c))
        def _():
            relay(sweep, c).wait_send()

    def exchange(stage, side, c):
        at = (part if stage % 2 else fine)(c)
        return pltpu.make_async_remote_copy(
            w.at[stage, :, at, :],
            halo.at[stage, side, :, at, :],
            halo_send.at[stage, side, c],
            halo_recv.at[stage, side, c],
            device_id=(t, (right, left)[side]),
            device_id_type=MESH,
        )

    def loop(body, count=PARTS):
        lax.fori_loop(0, count, lambda c, _: (body(c), 0)[1], 0)

    loop(lambda c: give(0, c), FINE)

    for load in loads:
        load.wait()

    def prepare(c, first, middle, last):
        rhs = [reaction(first), reaction(middle), reaction(last)]
        old = (first, middle, last)
        at = (slice(None), part(c), slice(None))
        r1[at] = sum(k * v for k, v in zip(FIRST, old))
        m1[at] = sum(k * v for k, v in zip(FIRST, rhs))
        r2[at] = sum(k * v for k, v in zip(SECOND, old))
        m2[at] = sum(k * v for k, v in zip(SECOND, rhs))

    def across(stage, c):
        here = w[stage, :, part(c), :]
        before = halo[stage, 0, :, part(c), :]
        after = halo[stage, 1, :, part(c), :]
        one = 16.0 * (before[1] + here[1]) - 30.0 * here[0] - (before[0] + after[0])
        two = 16.0 * (here[0] + after[0]) - 30.0 * here[1] - (before[1] + after[1])
        return jnp.stack([one, two]) * (1.0 / 12.0)

    def offer(stage, c, value):
        at = (part if stage % 2 else fine)(c)
        w[stage, :, at, :] = value
        exchange(stage, 0, c).start()
        exchange(stage, 1, c).start()
        high, low = split(value)
        w_high[:, at, :] = high
        w_low[:, at, :] = low

    def product_columns(c, count):
        at = pl.ds(pl.multiple_of(c * count, count), count)
        high = w_high[:, at, :].reshape(planes * count, nz)
        low = w_low[:, at, :].reshape(planes * count, nz)
        product = dot(high, q_high[...]) + dot(low, q_high[...]) + dot(high, q_low[...])
        qterm[:, at, :] = product.reshape(planes, count, nz)

    def product_rows():
        for p in range(planes):
            qterm[p] += (
                dot(q_high[...], w_high[p])
                + dot(q_high[...], w_low[p])
                + dot(q_low[...], w_high[p])
            )

    def arrive(stage, c):
        for i in [c] if stage % 2 else [ratio * c + i for i in range(ratio)]:
            exchange(stage, 0, i).wait_recv()
            exchange(stage, 1, i).wait_recv()

    loop(
        lambda c: prepare(
            c, u0[:, part(c), :], u1[:, part(c), :], u2[:, part(c), :]
        )
    )

    for sweep in range(2):
        begin = (a0, b0)[sweep]
        one, two = 2 * sweep, 2 * sweep + 1

        @pl.when(t == 0)
        def _():
            starts[sweep].wait()

        if sweep == 0:
            for k in range(0, 3 * PARTS // 4, 2):
                pass_on(0, k, True)

        def take(c):
            @pl.when(t > 0)
            def _():
                relay(sweep, c).wait_recv()

            value = begin[:, fine(c), :]
            if sweep == 1:
                out[0, 0, :, fine(c), :] = value
            base[:, fine(c), :] = value + HALF * reaction(value) + m1[:, fine(c), :]
            offer(one, c, HALF * value + r1[:, fine(c), :])
            product_columns(c, fine_rows)

        loop(take, FINE)
        product_rows()

        def middle(c):
            arrive(one, c)
            value = base[:, part(c), :] + qterm[:, part(c), :] + across(one, c)
            if sweep == 0:
                u1[:, part(c), :] = value
            else:
                out[0, 1, :, part(c), :] = value
            base[:, part(c), :] = value + HALF * reaction(value) + m2[:, part(c), :]
            offer(two, c, HALF * value + r2[:, part(c), :])

        loop(middle)
        product_columns(0, ny)
        product_rows()

        def final(c):
            if sweep == 0:
                pass_on(1, c - 4, (c >= 4) & (lax.rem(c, 2) == 0))
            arrive(two, c)
            value = base[:, part(c), :] + qterm[:, part(c), :] + across(two, c)
            if sweep == 0:
                u2[:, part(c), :] = value

                for i in range(ratio):
                    give(1, ratio * c + i)
                prepare(c, a0[:, part(c), :], u1[:, part(c), :], value)
            else:
                out[0, 2, :, part(c), :] = value

        if sweep == 0:
            loop(lambda c: given(0, c), FINE)

        loop(final)
        if sweep == 0:
            pass_on(1, PARTS - 4, True)

    for stage in range(4):

        def drain(c):
            exchange(stage, 0, c).wait_send()
            exchange(stage, 1, c).wait_send()

        loop(drain, PARTS if stage % 2 else FINE)

    loop(lambda c: given(1, c), FINE)


def solution(mesh):
    nt, ng = mesh.shape["tm"], mesh.shape["gx"]

    def local(initial, nodes):
        planes, ny, nz = initial.shape
        exact = second_derivative(ny).astype(np.float32)
        q_high = exact.astype(jnp.bfloat16)
        q_low = (exact - q_high.astype(np.float32)).astype(jnp.bfloat16)
        field = pltpu.VMEM((planes, ny, nz), jnp.float32)
        half_field = pltpu.VMEM((planes, ny, nz), jnp.bfloat16)
        dma = pltpu.SemaphoreType.DMA
        hbm = pl.BlockSpec(memory_space=pl.ANY)

        def body(*refs):
            kernel(nt, ng, *refs)

        return pl.pallas_call(
            body,
            out_shape=jax.ShapeDtypeStruct(nodes.shape, nodes.dtype),
            in_specs=[hbm, hbm, hbm, hbm],
            out_specs=pl.BlockSpec(memory_space=pltpu.VMEM),
            scratch_shapes=[
                field,
                field,
                field,
                field,
                field,
                pltpu.VMEM((2, planes, ny, nz), jnp.float32),
                pltpu.VMEM((4, planes, ny, nz), jnp.float32),
                pltpu.VMEM((4, 2, planes, ny, nz), jnp.float32),
                half_field,
                half_field,
                pltpu.VMEM((ny, ny), jnp.bfloat16),
                pltpu.VMEM((ny, ny), jnp.bfloat16),
                field,
                field,
                field,
                field,
                field,
                field,
                dma((5,)),
                dma((2,)),
                dma((2, FINE)),
                dma((2, FINE)),
                dma((2, FINE)),
                dma((4, 2, FINE)),
                dma((4, 2, FINE)),
            ],
            compiler_params=pltpu.CompilerParams(
                collective_id=0,
                has_side_effects=True,
                vmem_limit_bytes=24 * 1024 * 1024,
            ),
            name="sweeps",
        )(*(pltpu.with_memory_space_constraint(x, pltpu.HBM) for x in (initial, nodes, jnp.asarray(q_high), jnp.asarray(q_low))))

    in_specs = (P("gx", None, None), P("tm", None, "gx", None, None))
    out_specs = P("tm", None, "gx", None, None)
    return jax.shard_map(
        local, mesh=mesh, in_specs=in_specs, out_specs=out_specs, check_vma=False
    )
```

```python
import math

import jax
import jax.numpy as jnp
import numpy as np
from jax import lax
from jax.experimental import pallas as pl
from jax.experimental.pallas import tpu as pltpu
from jax.sharding import PartitionSpec as P

MESH = pl.DeviceIdType.MESH

SPACING = 2.0
STEP = 0.2
HALF = 0.1
PARTS = 8
AROUND = ((0, 1, 3), (1,))
FINE = 8

FIRST = (-HALF + STEP * 5.0 / 24.0, STEP / 3.0, -STEP / 24.0)
SECOND = (-STEP / 24.0, -HALF + STEP / 3.0, STEP * 5.0 / 24.0)


def second_derivative(count):
    positions = np.arange(count)
    offset = positions[None, :] - positions[:, None]
    angle_step = 2.0 * math.pi / count
    parity = np.where(offset % 2 == 0, 1.0, -1.0)
    safe = np.where(offset == 0, 1, offset)
    off_value = -0.5 * parity / np.sin(safe * (angle_step / 2.0)) ** 2
    diagonal = -(math.pi**2) / (3.0 * angle_step * angle_step) - 1.0 / 6.0
    return np.where(offset == 0, diagonal, off_value) * (angle_step / SPACING) ** 2


def split(x):
    high = x.astype(jnp.bfloat16)
    low = (x - high.astype(jnp.float32)).astype(jnp.bfloat16)
    return high, low


def dot(a, b):
    return jnp.dot(a, b, preferred_element_type=jnp.float32)


def reaction(v):
    return v - v * v * v


def kernel(
    nt,
    ng,
    initial,
    nodes,
    q_high_in,
    q_low_in,
    out,
    u0,
    u1,
    u2,
    a0,
    b0,
    passing,
    w,
    halo,
    w_high,
    w_low,
    q_high,
    q_low,
    r1,
    m1,
    r2,
    m2,
    base,
    qterm,
    load_sem,
    start_sem,
    relay_send,
    relay_recv,
    pass_recv,
    halo_send,
    halo_recv,
):
    t = lax.axis_index("tm")
    g = lax.axis_index("gx")
    right = lax.rem(g + 1, ng)
    left = lax.rem(g + ng - 1, ng)
    planes, ny, nz = u0.shape
    rows, fine_rows = ny // PARTS, ny // FINE
    ratio = FINE // PARTS
    turn = nt // 2

    def part(c):
        return pl.ds(pl.multiple_of(c * rows, rows), rows)

    def fine(c):
        return pl.ds(pl.multiple_of(c * fine_rows, fine_rows), fine_rows)

    loads = [
        pltpu.make_async_copy(nodes.at[0, m], u, load_sem.at[m])
        for m, u in enumerate((u0, u1, u2))
    ]
    loads += [
        pltpu.make_async_copy(q_high_in, q_high, load_sem.at[3]),
        pltpu.make_async_copy(q_low_in, q_low, load_sem.at[4]),
    ]
    for load in loads:
        load.start()

    starts = [
        pltpu.make_async_copy(initial, a, start_sem.at[i])
        for i, a in enumerate((a0, b0))
    ]

    @pl.when(t == 0)
    def _():
        for start in starts:
            start.start()

    barrier = pltpu.get_barrier_semaphore()
    for side in (left, right):
        pl.semaphore_signal(barrier, inc=1, device_id=(t, side), device_id_type=MESH)

    @pl.when(t > 0)
    def _():
        pl.semaphore_signal(barrier, inc=1, device_id=(t - 1, g), device_id_type=MESH)

    @pl.when(t == turn)
    def _():
        pl.semaphore_signal(barrier, inc=1, device_id=(nt - 1, g), device_id_type=MESH)

    @pl.when(t == nt - 1)
    def _():
        pl.semaphore_signal(barrier, inc=1, device_id=(turn - 1, g), device_id_type=MESH)

    pl.semaphore_wait(barrier, jnp.where(t == turn - 1, 4, 3))

    def relay(sweep, c):
        source = nodes.at[0, 2, :, fine(c), :] if sweep == 0 else u2.at[:, fine(c), :]
        target = (a0, b0)[sweep].at[:, fine(c), :]
        return pltpu.make_async_remote_copy(
            source,
            target,
            relay_send.at[sweep, c],
            relay_recv.at[sweep, c],
            device_id=(t + 1, g),
            device_id_type=MESH,
        )

    def detour(sweep, c):
        source = nodes.at[0, 2, :, fine(c), :] if sweep == 0 else u2.at[:, fine(c), :]
        return pltpu.make_async_remote_copy(
            source,
            passing.at[sweep, :, fine(c), :],
            relay_send.at[sweep, c],
            pass_recv.at[sweep, c],
            device_id=(nt - 1, g),
            device_id_type=MESH,
        )

    def forward(sweep, c):
        return pltpu.make_async_remote_copy(
            passing.at[sweep, :, fine(c), :],
            (a0, b0)[sweep].at[:, fine(c), :],
            relay_send.at[sweep, c],
            relay_recv.at[sweep, c],
            device_id=(turn, g),
            device_id_type=MESH,
        )

    def aside(sweep, c):
        found = c == -99
        for k in AROUND[sweep]:
            found = found | (c == k)
        return found

    def give(sweep, c):
        around = (t == turn - 1) & aside(sweep, c)

        @pl.when(around)
        def _():
            detour(sweep, c).start()

        @pl.when((t < nt - 1) & ~around)
        def _():
            relay(sweep, c).start()

    def pass_on(sweep, k, due):
        @pl.when((t == nt - 1) & due)
        def _():
            for i in range(ratio):
                detour(sweep, k * ratio + i).wait_recv()
                forward(sweep, k * ratio + i).start()

    def given(sweep, c):
        @pl.when((t < nt - 1) | aside(sweep, c))
        def _():
            relay(sweep, c).wait_send()

    def exchange(stage, side, c):
        at = (part if stage % 2 else fine)(c)
        return pltpu.make_async_remote_copy(
            w.at[stage, :, at, :],
            halo.at[stage, side, :, at, :],
            halo_send.at[stage, side, c],
            halo_recv.at[stage, side, c],
            device_id=(t, (right, left)[side]),
            device_id_type=MESH,
        )

    def loop(body, count=PARTS):
        lax.fori_loop(0, count, lambda c, _: (body(c), 0)[1], 0)

    loop(lambda c: give(0, c), FINE)

    for load in loads:
        load.wait()

    def prepare(c, first, middle, last):
        rhs = [reaction(first), reaction(middle), reaction(last)]
        old = (first, middle, last)
        at = (slice(None), part(c), slice(None))
        r1[at] = sum(k * v for k, v in zip(FIRST, old))
        m1[at] = sum(k * v for k, v in zip(FIRST, rhs))
        r2[at] = sum(k * v for k, v in zip(SECOND, old))
        m2[at] = sum(k * v for k, v in zip(SECOND, rhs))

    def across(stage, c):
        here = w[stage, :, part(c), :]
        before = halo[stage, 0, :, part(c), :]
        after = halo[stage, 1, :, part(c), :]
        one = 16.0 * (before[1] + here[1]) - 30.0 * here[0] - (before[0] + after[0])
        two = 16.0 * (here[0] + after[0]) - 30.0 * here[1] - (before[1] + after[1])
        return jnp.stack([one, two]) * (1.0 / 12.0)

    def offer(stage, c, value):
        at = (part if stage % 2 else fine)(c)
        w[stage, :, at, :] = value
        exchange(stage, 0, c).start()
        exchange(stage, 1, c).start()
        high, low = split(value)
        w_high[:, at, :] = high
        w_low[:, at, :] = low

    def product_columns(c, count):
        at = pl.ds(pl.multiple_of(c * count, count), count)
        high = w_high[:, at, :].reshape(planes * count, nz)
        low = w_low[:, at, :].reshape(planes * count, nz)
        product = dot(high, q_high[...]) + dot(low, q_high[...]) + dot(high, q_low[...])
        qterm[:, at, :] = product.reshape(planes, count, nz)

    def product_rows():
        for p in range(planes):
            qterm[p] += (
                dot(q_high[...], w_high[p])
                + dot(q_high[...], w_low[p])
                + dot(q_low[...], w_high[p])
            )

    def arrive(stage, c):
        for i in [c] if stage % 2 else [ratio * c + i for i in range(ratio)]:
            exchange(stage, 0, i).wait_recv()
            exchange(stage, 1, i).wait_recv()

    loop(
        lambda c: prepare(
            c, u0[:, part(c), :], u1[:, part(c), :], u2[:, part(c), :]
        )
    )

    for sweep in range(2):
        begin = (a0, b0)[sweep]
        one, two = 2 * sweep, 2 * sweep + 1

        @pl.when(t == 0)
        def _():
            starts[sweep].wait()

        if sweep == 0:
            for k in AROUND[0]:
                pass_on(0, k, True)

        def take(c):
            @pl.when(t > 0)
            def _():
                relay(sweep, c).wait_recv()

            value = begin[:, fine(c), :]
            if sweep == 1:
                out[0, 0, :, fine(c), :] = value
            base[:, fine(c), :] = value + HALF * reaction(value) + m1[:, fine(c), :]
            offer(one, c, HALF * value + r1[:, fine(c), :])
            product_columns(c, fine_rows)

        loop(take, FINE)
        product_rows()

        def middle(c):
            arrive(one, c)
            value = base[:, part(c), :] + qterm[:, part(c), :] + across(one, c)
            if sweep == 0:
                u1[:, part(c), :] = value
            else:
                out[0, 1, :, part(c), :] = value
            base[:, part(c), :] = value + HALF * reaction(value) + m2[:, part(c), :]
            offer(two, c, HALF * value + r2[:, part(c), :])

        loop(middle)
        product_columns(0, ny)
        product_rows()

        def final(c):
            if sweep == 0:
                pass_on(1, c - 4, aside(1, c - 4))
            arrive(two, c)
            value = base[:, part(c), :] + qterm[:, part(c), :] + across(two, c)
            if sweep == 0:
                u2[:, part(c), :] = value

                for i in range(ratio):
                    give(1, ratio * c + i)
                prepare(c, a0[:, part(c), :], u1[:, part(c), :], value)
            else:
                out[0, 2, :, part(c), :] = value

        if sweep == 0:
            loop(lambda c: given(0, c), FINE)

        loop(final)
        if sweep == 0:
            for k in AROUND[1]:
                if k >= PARTS - 4:
                    pass_on(1, k, True)

    for stage in range(4):

        def drain(c):
            exchange(stage, 0, c).wait_send()
            exchange(stage, 1, c).wait_send()

        loop(drain, PARTS if stage % 2 else FINE)

    loop(lambda c: given(1, c), FINE)


def solution(mesh):
    nt, ng = mesh.shape["tm"], mesh.shape["gx"]

    def local(initial, nodes):
        planes, ny, nz = initial.shape
        exact = second_derivative(ny).astype(np.float32)
        q_high = exact.astype(jnp.bfloat16)
        q_low = (exact - q_high.astype(np.float32)).astype(jnp.bfloat16)
        field = pltpu.VMEM((planes, ny, nz), jnp.float32)
        half_field = pltpu.VMEM((planes, ny, nz), jnp.bfloat16)
        dma = pltpu.SemaphoreType.DMA
        hbm = pl.BlockSpec(memory_space=pl.ANY)

        def body(*refs):
            kernel(nt, ng, *refs)

        return pl.pallas_call(
            body,
            out_shape=jax.ShapeDtypeStruct(nodes.shape, nodes.dtype),
            in_specs=[hbm, hbm, hbm, hbm],
            out_specs=pl.BlockSpec(memory_space=pltpu.VMEM),
            scratch_shapes=[
                field,
                field,
                field,
                field,
                field,
                pltpu.VMEM((2, planes, ny, nz), jnp.float32),
                pltpu.VMEM((4, planes, ny, nz), jnp.float32),
                pltpu.VMEM((4, 2, planes, ny, nz), jnp.float32),
                half_field,
                half_field,
                pltpu.VMEM((ny, ny), jnp.bfloat16),
                pltpu.VMEM((ny, ny), jnp.bfloat16),
                field,
                field,
                field,
                field,
                field,
                field,
                dma((5,)),
                dma((2,)),
                dma((2, FINE)),
                dma((2, FINE)),
                dma((2, FINE)),
                dma((4, 2, FINE)),
                dma((4, 2, FINE)),
            ],
            compiler_params=pltpu.CompilerParams(
                collective_id=0,
                has_side_effects=True,
                vmem_limit_bytes=24 * 1024 * 1024,
            ),
            name="sweeps",
        )(*(pltpu.with_memory_space_constraint(x, pltpu.HBM) for x in (initial, nodes, jnp.asarray(q_high), jnp.asarray(q_low))))

    in_specs = (P("gx", None, None), P("tm", None, "gx", None, None))
    out_specs = P("tm", None, "gx", None, None)
    return jax.shard_map(
        local, mesh=mesh, in_specs=in_specs, out_specs=out_specs, check_vma=False
    )
```

```python
import math

import jax
import jax.numpy as jnp
import numpy as np
from jax import lax
from jax.experimental import pallas as pl
from jax.experimental.pallas import tpu as pltpu
from jax.sharding import PartitionSpec as P

MESH = pl.DeviceIdType.MESH

SPACING = 2.0
STEP = 0.2
HALF = 0.1
PARTS = 8
AROUND = ((0, 1, 2, 3), (1,))
FINE = 8

FIRST = (-HALF + STEP * 5.0 / 24.0, STEP / 3.0, -STEP / 24.0)
SECOND = (-STEP / 24.0, -HALF + STEP / 3.0, STEP * 5.0 / 24.0)


def second_derivative(count):
    positions = np.arange(count)
    offset = positions[None, :] - positions[:, None]
    angle_step = 2.0 * math.pi / count
    parity = np.where(offset % 2 == 0, 1.0, -1.0)
    safe = np.where(offset == 0, 1, offset)
    off_value = -0.5 * parity / np.sin(safe * (angle_step / 2.0)) ** 2
    diagonal = -(math.pi**2) / (3.0 * angle_step * angle_step) - 1.0 / 6.0
    return np.where(offset == 0, diagonal, off_value) * (angle_step / SPACING) ** 2


def split(x):
    high = x.astype(jnp.bfloat16)
    low = (x - high.astype(jnp.float32)).astype(jnp.bfloat16)
    return high, low


def dot(a, b):
    return jnp.dot(a, b, preferred_element_type=jnp.float32)


def reaction(v):
    return v - v * v * v


def kernel(
    nt,
    ng,
    initial,
    nodes,
    q_high_in,
    q_low_in,
    out,
    u0,
    u1,
    u2,
    a0,
    b0,
    passing,
    w,
    halo,
    w_high,
    w_low,
    q_high,
    q_low,
    r1,
    m1,
    r2,
    m2,
    base,
    qterm,
    load_sem,
    start_sem,
    relay_send,
    relay_recv,
    pass_recv,
    halo_send,
    halo_recv,
):
    t = lax.axis_index("tm")
    g = lax.axis_index("gx")
    right = lax.rem(g + 1, ng)
    left = lax.rem(g + ng - 1, ng)
    planes, ny, nz = u0.shape
    rows, fine_rows = ny // PARTS, ny // FINE
    ratio = FINE // PARTS
    turn = nt // 2

    def part(c):
        return pl.ds(pl.multiple_of(c * rows, rows), rows)

    def fine(c):
        return pl.ds(pl.multiple_of(c * fine_rows, fine_rows), fine_rows)

    loads = [
        pltpu.make_async_copy(nodes.at[0, m], u, load_sem.at[m])
        for m, u in enumerate((u0, u1, u2))
    ]
    loads += [
        pltpu.make_async_copy(q_high_in, q_high, load_sem.at[3]),
        pltpu.make_async_copy(q_low_in, q_low, load_sem.at[4]),
    ]
    for load in loads:
        load.start()

    starts = [
        pltpu.make_async_copy(initial, a, start_sem.at[i])
        for i, a in enumerate((a0, b0))
    ]

    @pl.when(t == 0)
    def _():
        for start in starts:
            start.start()

    barrier = pltpu.get_barrier_semaphore()
    for side in (left, right):
        pl.semaphore_signal(barrier, inc=1, device_id=(t, side), device_id_type=MESH)

    @pl.when(t > 0)
    def _():
        pl.semaphore_signal(barrier, inc=1, device_id=(t - 1, g), device_id_type=MESH)

    @pl.when(t == turn)
    def _():
        pl.semaphore_signal(barrier, inc=1, device_id=(nt - 1, g), device_id_type=MESH)

    @pl.when(t == nt - 1)
    def _():
        pl.semaphore_signal(barrier, inc=1, device_id=(turn - 1, g), device_id_type=MESH)

    pl.semaphore_wait(barrier, jnp.where(t == turn - 1, 4, 3))

    def relay(sweep, c):
        source = nodes.at[0, 2, :, fine(c), :] if sweep == 0 else u2.at[:, fine(c), :]
        target = (a0, b0)[sweep].at[:, fine(c), :]
        return pltpu.make_async_remote_copy(
            source,
            target,
            relay_send.at[sweep, c],
            relay_recv.at[sweep, c],
            device_id=(t + 1, g),
            device_id_type=MESH,
        )

    def detour(sweep, c):
        source = nodes.at[0, 2, :, fine(c), :] if sweep == 0 else u2.at[:, fine(c), :]
        return pltpu.make_async_remote_copy(
            source,
            passing.at[sweep, :, fine(c), :],
            relay_send.at[sweep, c],
            pass_recv.at[sweep, c],
            device_id=(nt - 1, g),
            device_id_type=MESH,
        )

    def forward(sweep, c):
        return pltpu.make_async_remote_copy(
            passing.at[sweep, :, fine(c), :],
            (a0, b0)[sweep].at[:, fine(c), :],
            relay_send.at[sweep, c],
            relay_recv.at[sweep, c],
            device_id=(turn, g),
            device_id_type=MESH,
        )

    def aside(sweep, c):
        found = c == -99
        for k in AROUND[sweep]:
            found = found | (c == k)
        return found

    def give(sweep, c):
        around = (t == turn - 1) & aside(sweep, c)

        @pl.when(around)
        def _():
            detour(sweep, c).start()

        @pl.when((t < nt - 1) & ~around)
        def _():
            relay(sweep, c).start()

    def pass_on(sweep, k, due):
        @pl.when((t == nt - 1) & due)
        def _():
            for i in range(ratio):
                detour(sweep, k * ratio + i).wait_recv()
                forward(sweep, k * ratio + i).start()

    def given(sweep, c):
        @pl.when((t < nt - 1) | aside(sweep, c))
        def _():
            relay(sweep, c).wait_send()

    def exchange(stage, side, c):
        at = (part if stage % 2 else fine)(c)
        return pltpu.make_async_remote_copy(
            w.at[stage, :, at, :],
            halo.at[stage, side, :, at, :],
            halo_send.at[stage, side, c],
            halo_recv.at[stage, side, c],
            device_id=(t, (right, left)[side]),
            device_id_type=MESH,
        )

    def loop(body, count=PARTS):
        lax.fori_loop(0, count, lambda c, _: (body(c), 0)[1], 0)

    loop(lambda c: give(0, c), FINE)

    for load in loads:
        load.wait()

    def prepare(c, first, middle, last):
        rhs = [reaction(first), reaction(middle), reaction(last)]
        old = (first, middle, last)
        at = (slice(None), part(c), slice(None))
        r1[at] = sum(k * v for k, v in zip(FIRST, old))
        m1[at] = sum(k * v for k, v in zip(FIRST, rhs))
        r2[at] = sum(k * v for k, v in zip(SECOND, old))
        m2[at] = sum(k * v for k, v in zip(SECOND, rhs))

    def across(stage, c):
        here = w[stage, :, part(c), :]
        before = halo[stage, 0, :, part(c), :]
        after = halo[stage, 1, :, part(c), :]
        one = 16.0 * (before[1] + here[1]) - 30.0 * here[0] - (before[0] + after[0])
        two = 16.0 * (here[0] + after[0]) - 30.0 * here[1] - (before[1] + after[1])
        return jnp.stack([one, two]) * (1.0 / 12.0)

    def offer(stage, c, value):
        at = (part if stage % 2 else fine)(c)
        w[stage, :, at, :] = value
        exchange(stage, 0, c).start()
        exchange(stage, 1, c).start()
        high, low = split(value)
        w_high[:, at, :] = high
        w_low[:, at, :] = low

    def product_columns(c, count):
        at = pl.ds(pl.multiple_of(c * count, count), count)
        high = w_high[:, at, :].reshape(planes * count, nz)
        low = w_low[:, at, :].reshape(planes * count, nz)
        product = dot(high, q_high[...]) + dot(low, q_high[...]) + dot(high, q_low[...])
        qterm[:, at, :] = product.reshape(planes, count, nz)

    def product_rows():
        for p in range(planes):
            qterm[p] += (
                dot(q_high[...], w_high[p])
                + dot(q_high[...], w_low[p])
                + dot(q_low[...], w_high[p])
            )

    def arrive(stage, c):
        for i in [c] if stage % 2 else [ratio * c + i for i in range(ratio)]:
            exchange(stage, 0, i).wait_recv()
            exchange(stage, 1, i).wait_recv()

    loop(
        lambda c: prepare(
            c, u0[:, part(c), :], u1[:, part(c), :], u2[:, part(c), :]
        )
    )

    for sweep in range(2):
        begin = (a0, b0)[sweep]
        one, two = 2 * sweep, 2 * sweep + 1

        @pl.when(t == 0)
        def _():
            starts[sweep].wait()

        if sweep == 0:
            for k in AROUND[0]:
                pass_on(0, k, True)

        def take(c):
            @pl.when(t > 0)
            def _():
                relay(sweep, c).wait_recv()

            value = begin[:, fine(c), :]
            if sweep == 1:
                out[0, 0, :, fine(c), :] = value
            base[:, fine(c), :] = value + HALF * reaction(value) + m1[:, fine(c), :]
            offer(one, c, HALF * value + r1[:, fine(c), :])
            product_columns(c, fine_rows)

        loop(take, FINE)
        product_rows()

        def middle(c):
            arrive(one, c)
            value = base[:, part(c), :] + qterm[:, part(c), :] + across(one, c)
            if sweep == 0:
                u1[:, part(c), :] = value
            else:
                out[0, 1, :, part(c), :] = value
            base[:, part(c), :] = value + HALF * reaction(value) + m2[:, part(c), :]
            offer(two, c, HALF * value + r2[:, part(c), :])

        loop(middle)
        product_columns(0, ny)
        product_rows()

        def final(c):
            if sweep == 0:
                pass_on(1, c - 4, aside(1, c - 4))
            arrive(two, c)
            value = base[:, part(c), :] + qterm[:, part(c), :] + across(two, c)
            if sweep == 0:
                u2[:, part(c), :] = value

                for i in range(ratio):
                    give(1, ratio * c + i)
                prepare(c, a0[:, part(c), :], u1[:, part(c), :], value)
            else:
                out[0, 2, :, part(c), :] = value

        if sweep == 0:
            loop(lambda c: given(0, c), FINE)

        loop(final)
        if sweep == 0:
            for k in AROUND[1]:
                if k >= PARTS - 4:
                    pass_on(1, k, True)

    for stage in range(4):

        def drain(c):
            exchange(stage, 0, c).wait_send()
            exchange(stage, 1, c).wait_send()

        loop(drain, PARTS if stage % 2 else FINE)

    loop(lambda c: given(1, c), FINE)


def solution(mesh):
    nt, ng = mesh.shape["tm"], mesh.shape["gx"]

    def local(initial, nodes):
        planes, ny, nz = initial.shape
        exact = second_derivative(ny).astype(np.float32)
        q_high = exact.astype(jnp.bfloat16)
        q_low = (exact - q_high.astype(np.float32)).astype(jnp.bfloat16)
        field = pltpu.VMEM((planes, ny, nz), jnp.float32)
        half_field = pltpu.VMEM((planes, ny, nz), jnp.bfloat16)
        dma = pltpu.SemaphoreType.DMA
        hbm = pl.BlockSpec(memory_space=pl.ANY)

        def body(*refs):
            kernel(nt, ng, *refs)

        return pl.pallas_call(
            body,
            out_shape=jax.ShapeDtypeStruct(nodes.shape, nodes.dtype),
            in_specs=[hbm, hbm, hbm, hbm],
            out_specs=pl.BlockSpec(memory_space=pltpu.VMEM),
            scratch_shapes=[
                field,
                field,
                field,
                field,
                field,
                pltpu.VMEM((2, planes, ny, nz), jnp.float32),
                pltpu.VMEM((4, planes, ny, nz), jnp.float32),
                pltpu.VMEM((4, 2, planes, ny, nz), jnp.float32),
                half_field,
                half_field,
                pltpu.VMEM((ny, ny), jnp.bfloat16),
                pltpu.VMEM((ny, ny), jnp.bfloat16),
                field,
                field,
                field,
                field,
                field,
                field,
                dma((5,)),
                dma((2,)),
                dma((2, FINE)),
                dma((2, FINE)),
                dma((2, FINE)),
                dma((4, 2, FINE)),
                dma((4, 2, FINE)),
            ],
            compiler_params=pltpu.CompilerParams(
                collective_id=0,
                has_side_effects=True,
                vmem_limit_bytes=24 * 1024 * 1024,
            ),
            name="sweeps",
        )(*(pltpu.with_memory_space_constraint(x, pltpu.HBM) for x in (initial, nodes, jnp.asarray(q_high), jnp.asarray(q_low))))

    in_specs = (P("gx", None, None), P("tm", None, "gx", None, None))
    out_specs = P("tm", None, "gx", None, None)
    return jax.shard_map(
        local, mesh=mesh, in_specs=in_specs, out_specs=out_specs, check_vma=False
    )
```
